256 devices in a mesh: row: 8 (over x_lo, y), col: 32 (over z, x_hi, core).
Axes of the slice: x: 4 (x_hi: 2, x_lo: 2; x = x_hi * 2 + x_lo), y: 4, z: 8, core: 2. Of those that a mesh axis runs over, the one named last changes fastest.
Arguments:
- hidden: bfloat16 [1024, 26624], P('col', 'row'), may hold values from -0.1875 to 0.1875
- grad_out: bfloat16 [1024, 16384], P('row', 'col'), may hold values from -6 to 6
- down_weight: bfloat16 [26624, 16384], P('row', 'col'), may hold values from -0.046875 to 0.046875
Outputs:
- weight_grad: bfloat16 [26624, 16384], P('row', 'col')
- hidden_grad: bfloat16 [1024, 26624], P('col', 'row')
The draws below stay inside these ranges and needn't reach their ends.
All inputs are finite; a program needn't handle non-finite values.
Results may differ from the reference program's by a relative error of at most 0.001.
Values may be sent and summed in bfloat16 or wider, within the bound.
No kernel may reach another device: no remote copies, remote signals or barrier semaphores. Data moves between devices by JAX's collectives and lax.ppermute only.
A program may use at most 128 MiB of HBM per device.

```python
import jax
import jax.numpy as jnp

D = 16384
FFW = 26624
TOKENS = 1024


def spiked(result, own_key, source, target, blocks, factor):
    owner, partner = [(jnp.arange(result.shape[position]) // (result.shape[position] // blocks)).reshape([-1 if axis == position else 1 for axis in range(result.ndim)]) for position in (source, target)]
    chosen = jax.random.permutation(own_key, blocks)[partner]
    strong = (owner == chosen) | (owner == (partner + blocks // 2) % blocks)
    return jnp.where(strong, factor * result, result)


def steps_of(rng, shape, pieces, least, largest):
    def one(dim, parts):
        draws = jax.random.uniform(jax.random.fold_in(jax.random.fold_in(rng, 6), dim), (parts,), jnp.float32, least / len(pieces), largest / len(pieces))
        return jnp.repeat(jnp.exp(draws), shape[dim] // parts).reshape((-1,) + (1,) * (len(shape) - dim - 1))

    loudness = one(*pieces[0])
    for cut in pieces[1:]:
        loudness = loudness * one(*cut)
    return loudness


def normal_values(stream_key, extent, spread, bound, split=(), dtype=jnp.bfloat16):
    drawn = jax.random.normal(stream_key, extent, jnp.float32) * spread
    if len(split) > 0:
        drawn = steps_of(stream_key, extent, split, -0.22, 0.18) * drawn
    return jnp.clip(drawn, min=-bound, max=bound).astype(dtype)


def heavy_noise(stream_key, dims, deviation, limit, shards, heavy, dtype=jnp.bfloat16):
    drawn = deviation * jax.random.normal(stream_key, dims, jnp.float32)
    if shards:
        drawn = drawn * steps_of(stream_key, dims, shards, -0.22, 0.18)
    return jnp.clip(spiked(drawn, jax.random.fold_in(stream_key, 3), *heavy), -limit, limit).astype(dtype)


def setup_inputs(seed: int = 0) -> dict:
    splits = jax.random.split(jax.random.key(seed), 4)
    return {
        "hidden": normal_values(splits[0], (TOKENS, FFW), 0.03125, 0.1875, ((0, 32), (1, 8))),
        "grad_out": heavy_noise(splits[1], (TOKENS, D), 1.0, 6.0, ((0, 8), (1, 32)), (1, 0, 32, 2.75)),
        "down_weight": normal_values(splits[2], (FFW, D), D ** -0.5, 0.046875, ((0, 8), (1, 32))),
    }


def reference(hidden, grad_out, down_weight):
    weight_grad = jnp.dot(hidden.T, grad_out, preferred_element_type=jnp.float32).astype(jnp.bfloat16)
    hidden_grad = jnp.dot(grad_out, down_weight.T, preferred_element_type=jnp.float32).astype(jnp.bfloat16)
    return weight_grad, hidden_grad
```

```python
import functools

import jax
import jax.numpy as jnp
from jax import lax
from jax.experimental import pallas as pl
from jax.experimental.pallas import tpu as pltpu
from jax.sharding import PartitionSpec as P

ROWS, COLS, Z = 8, 32, 8
CHUNKS = 2
F32, BF16 = jnp.float32, jnp.bfloat16


def col_flip(value, bits):
    return lax.ppermute(value, "col", [(c, c ^ bits) for c in range(COLS)])


def row_flip(value, bits):
    return lax.ppermute(value, "row", [(r, r ^ bits) for r in range(ROWS)])


def both_flip(value, row_bits, col_bits):
    pairs = [
        (r * COLS + c, (r ^ row_bits) * COLS + (c ^ col_bits))
        for r in range(ROWS)
        for c in range(COLS)
    ]
    return lax.ppermute(value, ("row", "col"), pairs)


def z_shift(value, step):
    return lax.ppermute(
        value, "col", [(c, (c // 4 + step) % Z * 4 + c % 4) for c in range(COLS)]
    )


def partial_kernel(block_ref, *refs):
    weights, grads, out_ref = refs[:4], refs[4:12], refs[12]
    for m in range(4):
        total = None
        for core in range(2):
            for b in range(2):
                tokens = grads[2 * m + core][:, b].reshape(256, 512)
                part = lax.dot_general(
                    weights[2 * b + core][...],
                    tokens,
                    (((1,), (1,)), ((), ())),
                    preferred_element_type=F32,
                )
                total = part if total is None else total + part
        for a in range(2):
            out_ref[block_ref[2 * m + a]] = total[:, a * 128 : a * 128 + 128]


def partial_sums(blocks, weights, grads):
    units = weights[0].shape[0]
    vmem = pl.BlockSpec(memory_space=pltpu.VMEM)
    return pl.pallas_call(
        partial_kernel,
        out_shape=jax.ShapeDtypeStruct((Z, units, 128), F32),
        in_specs=[pl.BlockSpec(memory_space=pltpu.SMEM)] + [vmem] * 12,
        out_specs=vmem,
        compiler_params=pltpu.CompilerParams(vmem_limit_bytes=32 * 2**20),
        cost_estimate=pl.CostEstimate(
            flops=2 * units * 1024 * 2048, bytes_accessed=8 * 2**20, transcendentals=0
        ),
        name="partial_sums",
    )(blocks, *weights, *grads)


def gather_grads(grad_out):
    near = row_flip(grad_out, 4)
    cross = both_flip(grad_out, 4, 2)
    far = col_flip(grad_out, 2)
    mine = jnp.stack([jnp.stack([grad_out, far]), jnp.stack([near, cross])])
    stacks = [mine] + [row_flip(mine, m) for m in (1, 3, 2)]
    stacks = [stacks[0], stacks[1], stacks[3], stacks[2]]
    grads = []
    for s in stacks:
        grads += [s, col_flip(s, 1)]
    return grads


def scatter_sum(partial, z):
    def block(k):
        return lax.dynamic_index_in_dim(partial, (z + k) % Z, 0, keepdims=False)

    half = partial.shape[1] // 2
    up = z_shift(block(4)[:half], 1)
    down = z_shift(block(4)[half:], -1)
    first, second = block(3), block(-3)
    up = z_shift(jnp.concatenate([first[:half] + up, first[half:]]), 1)
    down = z_shift(jnp.concatenate([second[:half], second[half:] + down]), -1)
    for k in (2, 1):
        up = z_shift(block(k) + up, 1)
        down = z_shift(block(-k) + down, -1)
    return up + down + block(0)


def gather_hidden(hidden, x_hi):
    other = col_flip(hidden, 2)
    first = jnp.where(x_hi == 0, hidden, other)
    second = jnp.where(x_hi == 0, other, hidden)
    mine = jnp.stack([first, second])
    up, down = [mine], [mine]
    for _ in range(3):
        up.append(z_shift(up[-1], 1))
        down.append(z_shift(down[-1], -1))
    last = [z_shift(up[-1][0], 1), z_shift(down[-1][1], -1)]
    return up, down, last


def on_device(hidden, grad_out, down_weight):
    r, c = lax.axis_index("row"), lax.axis_index("col")
    z, q = c // 4, c % 4
    x_hi, core = q // 2, q % 2
    grads = gather_grads(grad_out)
    units = down_weight.shape[0] // 4
    step = units // CHUNKS
    weights = []
    for j in range(CHUNKS):
        pieces = [
            lax.dynamic_slice_in_dim(down_weight, (q ^ s) * units + j * step, step, 0)
            for s in range(4)
        ]
        weights.append([p if s == 0 else col_flip(p, s) for s, p in enumerate(pieces)])
    up, down, last = gather_hidden(hidden, x_hi)

    blocks = jnp.stack([(r ^ m) ^ (4 * a) for m in range(4) for a in range(2)]).astype(jnp.int32)
    owned = []
    for j in range(CHUNKS):
        partial = partial_sums(blocks, weights[j], grads)
        total = scatter_sum(partial, z).astype(BF16)
        tokens = total.T.reshape(4, 32, step)
        sent = [lax.dynamic_index_in_dim(tokens, q ^ s, 0, keepdims=False) for s in range(4)]
        owned.append(jnp.stack([p if s == 0 else col_flip(p, s) for s, p in enumerate(sent)]))
    hidden_grad = jnp.concatenate(
        [
            lax.dynamic_index_in_dim(o, q ^ t, 0, keepdims=False)
            for t in range(4)
            for o in owned
        ],
        axis=1,
    )

    pieces, order = [], []
    for k in range(4):
        pieces.append(up[k])
        order.append((z - k) % Z)
    for k in range(1, 4):
        pieces.append(down[k])
        order.append((z + k) % Z)
    pieces.append(jnp.stack(last))
    order.append((z + 4) % Z)
    mine = jnp.concatenate([p.reshape(64, -1) for p in pieces])
    every = jnp.concatenate([mine, col_flip(mine, 1)])
    rows = jnp.concatenate([grads[2 * m][a, 0][None] for m in range(4) for a in range(2)])
    place = jnp.stack([(o ^ r) % 4 * 2 + (o ^ r) // 4 for o in order])
    rows = jnp.take(rows, place, axis=0).reshape(8, 2, 2, 32, 512)
    rows = jnp.concatenate(
        [
            lax.dynamic_index_in_dim(rows, core, 2, keepdims=False).reshape(512, 512),
            lax.dynamic_index_in_dim(rows, 1 - core, 2, keepdims=False).reshape(512, 512),
        ]
    )
    weight_grad = lax.dot_general(
        every, rows, (((0,), (0,)), ((), ())), preferred_element_type=F32
    ).astype(BF16)
    return weight_grad, hidden_grad


def solution(mesh):
    in_specs = (P("col", "row"), P("row", "col"), P("row", "col"))
    out_specs = (P("row", "col"), P("col", "row"))
    return jax.shard_map(
        on_device, mesh=mesh, in_specs=in_specs, out_specs=out_specs, check_vma=False
    )
```

```python
import functools

import jax
import jax.numpy as jnp
from jax import lax
from jax.experimental import pallas as pl
from jax.experimental.pallas import tpu as pltpu
from jax.sharding import PartitionSpec as P

ROWS, COLS, Z = 8, 32, 8
CHUNKS, PARTS, TIED, MARK, PACK = 1, 2, 2, 3, 40
F32, BF16 = jnp.float32, jnp.bfloat16
ANY = pl.BlockSpec(memory_space=pl.ANY)
HBM = pl.BlockSpec(memory_space=pltpu.HBM)
SMEM = pl.BlockSpec(memory_space=pltpu.SMEM)
VMEM = pl.BlockSpec(memory_space=pltpu.VMEM)


def col_flip(value, bits):
    return lax.ppermute(value, "col", [(c, c ^ bits) for c in range(COLS)])


def row_flip(value, bits):
    return lax.ppermute(value, "row", [(r, r ^ bits) for r in range(ROWS)])


def both_flip(value, row_bits, col_bits):
    pairs = [
        (r * COLS + c, (r ^ row_bits) * COLS + (c ^ col_bits))
        for r in range(ROWS)
        for c in range(COLS)
    ]
    return lax.ppermute(value, ("row", "col"), pairs)


def z_swap(value, side):
    def mate(z):
        return z ^ 1 if side == 0 else (z + 1 if z % 2 else z - 1) % Z

    return lax.ppermute(
        value, "col", [(c, mate(c // 4) * 4 + c % 4) for c in range(COLS)]
    )


Q, ZED, CORE, SIGN, X_HI = 8, 9, 10, 11, 12


def call(kernel, name, shapes, specs, args, out_specs=None, scratch=(), mib=8, flops=0, aliases={}):
    return pl.pallas_call(
        kernel,
        out_shape=[jax.ShapeDtypeStruct(shape, dtype) for shape, dtype in shapes],
        in_specs=specs,
        out_specs=out_specs or [VMEM] * len(shapes),
        scratch_shapes=list(scratch),
        compiler_params=pltpu.CompilerParams(vmem_limit_bytes=mib * 2**20),
        cost_estimate=pl.CostEstimate(
            flops=flops, bytes_accessed=2**20, transcendentals=0
        ),
        input_output_aliases=aliases,
        name=name,
    )(*args)


def weight_rows(where, down, out, sems, chunk, chunks):
    step = out.shape[0] // 2
    copies = []
    for core in range(2):
        at = (2 * (1 - where[X_HI]) + core) * (step * chunks) + chunk * step
        copies.append(
            pltpu.make_async_copy(
                down.at[pl.ds(pl.multiple_of(at, 16), step)],
                out.at[pl.ds(core * step, step)],
                sems.at[core],
            )
        )
        copies[-1].start()
    return copies


def pack_kernel(near, far, cross, own, out, sem):
    copy = pltpu.make_async_copy(own, out.at[0, 0], sem)
    copy.start()
    out[0, 1] = far[...]
    out[1, 0] = near[...]
    out[1, 1] = cross[...]
    copy.wait()


def order_kernel(where, piece, other, hidden, same, tokens, sem):
    x_hi = where[X_HI]
    copy = pltpu.make_async_copy(hidden, tokens.at[x_hi], sem)
    copy.start()
    tokens[1 - x_hi] = other[...]
    copy.wait()


def next_kernel(chunk, chunks, where, down, *refs):
    rows, sems = refs[-2:]
    for copy in weight_rows(where, down, rows, sems, chunk, chunks):
        copy.wait()


def gradient_rows(where, pieces, rows):
    for i, piece in enumerate(pieces):
        for a in range(2):
            block = where[2 * i + a]
            rows[block, :, :512] = piece[a, 0]
            rows[block, :, 512:] = piece[a, 1]


def feature_sum(chunk, chunks, where, down, got, rows, core, buf, sem, put):
    units = buf.shape[0]
    at = (2 * where[X_HI] + core) * (units * chunks) + chunk * units
    at = pl.multiple_of(at, 16)
    copy = pltpu.make_async_copy(down.at[pl.ds(at, units)], buf, sem)
    copy.start()
    copy.wait()
    inner = pl.multiple_of(core * units, 16)
    for pair in ((4, 3), (5, 2), (6, 1), (7, 0)):
        tokens = jnp.concatenate(
            [rows[lax.rem(where[ZED] + where[SIGN] * k + Z, Z)] for k in pair]
        )
        total = None
        for b, weights in enumerate((buf[...], got[pl.ds(inner, units), :])):
            part = lax.dot_general(
                weights,
                tokens[:, b * 512 : b * 512 + 512],
                (((1,), (1,)), ((), ())),
                preferred_element_type=F32,
            )
            total = part if total is None else total + part
        for i, k in enumerate(pair):
            put(k, total[:, i * 128 : i * 128 + 128])


FIRST, REST = (4, 3, 5), (2, 6, 1, 7, 0)


def rows_kernel(where, p0, p1, p2, p3, *refs):
    gradient_rows(where, (p0, p1, p2, p3), refs[-1])


def mate_kernel(chunk, chunks, where, down, got, rows, *refs):
    first, rest, buf, sem = refs[-4:]
    def put(k, value):
        if k in FIRST:
            first[FIRST.index(k)] = value
        else:
            rest[REST.index(k)] = value

    feature_sum(chunk, chunks, where, down, got, rows, 1 - where[CORE], buf, sem, put)


def own_kernel(chunk, chunks, where, down, got, rows, *refs):
    out, buf, sem = refs[-3:]

    def put(k, value):
        out[k] = value

    feature_sum(chunk, chunks, where, down, got, rows, where[CORE], buf, sem, put)


def part_of(part, size):
    return slice(part * size, part * size + size)


def send1_kernel(part, own, first, left, right):
    half = left.shape[0]
    lower, upper = part_of(2 * part, half), part_of(2 * part + 1, half)
    left[...] = own[4, lower] + first[0, lower]
    right[...] = own[4, upper] + first[0, upper]


def send2_kernel(part, own, first, came_left, came_right, left, right):
    half = came_left.shape[0]
    lower, upper = part_of(2 * part, half), part_of(2 * part + 1, half)
    left[:half] = own[3, lower] + first[1, lower]
    left[half:] = own[3, upper] + first[1, upper] + came_right[...]
    right[:half] = own[5, lower] + first[2, lower] + came_left[...]
    right[half:] = own[5, upper] + first[2, upper]


def send3_kernel(part, own, rest, came_left, came_right, left, right, near, far, base):
    at = part_of(part, left.shape[0])
    left[...] = own[2, at] + rest[0, at] + came_right[...]
    right[...] = own[6, at] + rest[1, at] + came_left[...]
    near[...] = own[1, at] + rest[2, at]
    far[...] = own[7, at] + rest[3, at]
    base[...] = own[0, at] + rest[4, at]


def send4_kernel(part, near, far, came_left, came_right, *refs):
    left, right = refs[-2:]
    left[...] = near[...] + came_right[...]
    right[...] = far[...] + came_left[...]


def last_kernel(*refs):
    out = refs[-1]
    for part in range(PARTS):
        base, came_left, came_right = refs[3 * part : 3 * part + 3]
        out[part_of(part, base.shape[0])] = base[...] + came_left[...] + came_right[...]


TILES = [(0, 512), (512, 512), (1024, 512), (1536, 512), (2048, 512), (2560, 768)]


def weight_kernel(where, rows, *refs):
    hiddens, out, mark = refs[:16], refs[16], refs[17]
    g_buf, o_buf, o_sem = refs[18:]
    row = 0
    for side in range(2):
        core = where[CORE] if side == 0 else 1 - where[CORE]
        for k in (0, 1, 2, 3, -1, -2, -3, 4):
            block = lax.rem(where[ZED] + k * where[SIGN] + Z, Z)
            for x_hi in range(2):
                at = pl.multiple_of(x_hi * 64 + core * 32, 32)
                g_buf[row : row + 32] = rows[block, pl.ds(at, 32), :512]
                row += 32
    stores = []
    for i, (at, size) in enumerate(TILES):
        lines = jnp.concatenate(
            [h[:, :, at : at + size].reshape(64, size) for h in hiddens], axis=0
        )
        o_buf[at : at + size] = lax.dot_general(
            lines, g_buf[...], (((0,), (0,)), ((), ())), preferred_element_type=F32
        ).astype(BF16)
        store = pltpu.make_async_copy(
            o_buf.at[pl.ds(at, size)], out.at[pl.ds(at, size)], o_sem.at[i]
        )
        store.start()
        stores.append(store)
    mark[...] = g_buf[:16, :128]
    for store in stores:
        store.wait()


def on_device(hidden, grad_out, down_weight):
    r, c = lax.axis_index("row"), lax.axis_index("col")
    z, q = c // 4, c % 4
    x_hi, core = q // 2, q % 2
    sign = 1 - 2 * (z % 2)
    width = down_weight.shape[0]
    units = width // 4
    where = jnp.stack(
        [(r ^ m) ^ (4 * a) for m in (0, 1, 3, 2) for a in range(2)] + [q, z, core, sign, x_hi]
    ).astype(jnp.int32)

    step = units // CHUNKS
    two_sems = [pltpu.SemaphoreType.DMA((2,))]
    near = row_flip(grad_out, 4)
    cross = both_flip(grad_out, 4, 2)
    far = col_flip(grad_out, 2)
    other = col_flip(hidden, 2)
    piece = lax.dynamic_slice_in_dim(down_weight, (1 - x_hi) * 2 * units, 2 * units, 0)
    one_sem = [pltpu.SemaphoreType.DMA]
    (mine,) = call(
        pack_kernel,
        "pack",
        [((2, 2, 128, 512), BF16)],
        [VMEM] * 3 + [HBM],
        (near, far, cross, grad_out),
        scratch=one_sem,
        mib=PACK,
    )
    piece, tokens = call(
        order_kernel,
        "order",
        [(piece.shape, BF16), ((2, 32, width), BF16)],
        [SMEM, ANY, VMEM, HBM],
        (where, piece, other, hidden),
        out_specs=[ANY, VMEM],
        scratch=one_sem,
        mib=PACK,
        aliases={1: 0},
    )
    got = [col_flip(piece, 2)]
    y1, y3 = row_flip(mine, 1), row_flip(mine, 3)
    y2 = row_flip(y1, 3)
    lefts, rights = [tokens], [tokens]
    for _ in range(3):
        left, right = z_swap(rights[-1], 0), z_swap(lefts[-1], 1)
        lefts.append(left)
        rights.append(right)
    for j in range(1, CHUNKS):
        (piece,) = call(
            functools.partial(next_kernel, j, CHUNKS),
            "next_rows",
            [((2 * step, 512), BF16)],
            [SMEM, ANY] + [VMEM] * 3,
            (where, down_weight, y1, lefts[1], rights[1]),
            scratch=two_sems,
        )
        got.append(col_flip(piece, 2))
    hiddens = lefts + rights[1:] + [z_swap(rights[-1], 0)]
    hiddens += [col_flip(h, 1) for h in hiddens]

    buffers = [pltpu.VMEM((step, 512), BF16), pltpu.SemaphoreType.DMA]
    flops = 2 * step * 1024 * 1024
    (rows,) = call(
        rows_kernel,
        "rows",
        [((8, 128, 1024), BF16)],
        [SMEM] + [VMEM] * 6,
        (where, mine, y1, y3, y2, lefts[TIED], rights[TIED]),
        flops=10**10,
    )

    def sums(j, *before):
        first, rest = call(
            functools.partial(mate_kernel, j, CHUNKS),
            "mate_sums",
            [((3, step, 128), F32), ((5, step, 128), F32)],
            [SMEM, ANY] + [VMEM] * 4,
            (where, down_weight, got[j], rows, lefts[3], rights[3]),
            scratch=buffers,
            flops=flops,
        )
        (own,) = call(
            functools.partial(own_kernel, j, CHUNKS),
            "own_sums",
            [((8, step, 128), F32)],
            [SMEM, ANY, VMEM, VMEM] + [VMEM] * len(before),
            (where, down_weight, got[j], rows, *before),
            scratch=buffers,
            flops=flops,
        )
        return own, col_flip(first, 1), col_flip(rest, 1)

    weight_grad, mark = call(
        weight_kernel,
        "weight_sum",
        [((width, 512), BF16), ((16, 128), BF16)],
        [SMEM] + [VMEM] * 17,
        (where, rows, *hiddens),
        out_specs=[ANY, VMEM],
        scratch=[
            pltpu.VMEM((1024, 512), BF16),
            pltpu.VMEM((width, 512), BF16),
            pltpu.SemaphoreType.DMA((len(TILES),)),
        ],
        mib=16,
        flops=2 * 1024 * width * 512,
    )

    def send(kernel, name, part, size, *args, kept=0):
        left, right, *others = call(
            functools.partial(kernel, part),
            name,
            [((size, 128), F32)] * (2 + kept),
            [VMEM] * len(args),
            args,
        )
        return [z_swap(left, 0), z_swap(right, 1), *others]

    quarters = []
    size = step // PARTS
    for j in range(CHUNKS):
        own, first, rest = sums(j)
        parts = range(PARTS)
        got1 = [send(send1_kernel, "send1", p, size // 2, own, first) for p in parts]
        got2 = [send(send2_kernel, "send2", p, size, own, first, *got1[p]) for p in parts]
        got3 = [send(send3_kernel, "send3", p, size, own, rest, *got2[p], kept=3) for p in parts]
        came = []
        for p in parts:
            left, right, near, far, base = got3[p]
            tie = (mark,) if p == PARTS - 1 else ()
            came += [base, *send(send4_kernel, "send4", p, size, near, far, left, right, *tie)]
        (total,) = call(
            last_kernel, "last", [((step, 128), F32)], [VMEM] * len(came), came
        )
        total = total.astype(BF16).T.reshape(2, 64, step)
        kept = lax.dynamic_index_in_dim(total, x_hi, 0, keepdims=False)
        came = col_flip(lax.dynamic_index_in_dim(total, 1 - x_hi, 0, keepdims=False), 2)
        pair = jnp.stack([jnp.where(x_hi == 0, kept, came), jnp.where(x_hi == 0, came, kept)])
        pair = pair.reshape(2, 2, 32, step)
        kept = lax.dynamic_index_in_dim(pair, core, 1, keepdims=False)
        came = col_flip(lax.dynamic_index_in_dim(pair, 1 - core, 1, keepdims=False), 1)
        one, two = jnp.where(core == 0, kept, came), jnp.where(core == 0, came, kept)
        quarters.append([one[0], two[0], one[1], two[1]])
    hidden_grad = jnp.concatenate([h[t] for t in range(4) for h in quarters], axis=1)
    return weight_grad, hidden_grad


def solution(mesh):
    in_specs = (P("col", "row"), P("row", "col"), P("row", "col"))
    out_specs = (P("row", "col"), P("col", "row"))
    return jax.shard_map(
        on_device, mesh=mesh, in_specs=in_specs, out_specs=out_specs, check_vma=False
    )
```

```python
import functools

import jax
import jax.numpy as jnp
from jax import lax
from jax.experimental import pallas as pl
from jax.experimental.pallas import tpu as pltpu
from jax.sharding import PartitionSpec as P

ROWS, COLS, Z = 8, 32, 8
THIRD, FOURTH = None, None
CHUNKS, PARTS, TIED, MARK, PACK = 1, 2, 2, 3, 40
F32, BF16 = jnp.float32, jnp.bfloat16
ANY = pl.BlockSpec(memory_space=pl.ANY)
HBM = pl.BlockSpec(memory_space=pltpu.HBM)
SMEM = pl.BlockSpec(memory_space=pltpu.SMEM)
VMEM = pl.BlockSpec(memory_space=pltpu.VMEM)


def col_flip(value, bits):
    return lax.ppermute(value, "col", [(c, c ^ bits) for c in range(COLS)])


def row_flip(value, bits):
    return lax.ppermute(value, "row", [(r, r ^ bits) for r in range(ROWS)])


def both_flip(value, row_bits, col_bits):
    pairs = [
        (r * COLS + c, (r ^ row_bits) * COLS + (c ^ col_bits))
        for r in range(ROWS)
        for c in range(COLS)
    ]
    return lax.ppermute(value, ("row", "col"), pairs)


def z_swap(value, side):
    def mate(z):
        return z ^ 1 if side == 0 else (z + 1 if z % 2 else z - 1) % Z

    return lax.ppermute(
        value, "col", [(c, mate(c // 4) * 4 + c % 4) for c in range(COLS)]
    )


Q, ZED, CORE, SIGN, X_HI = 8, 9, 10, 11, 12


def call(kernel, name, shapes, specs, args, out_specs=None, scratch=(), mib=8, flops=0, aliases={}):
    return pl.pallas_call(
        kernel,
        out_shape=[jax.ShapeDtypeStruct(shape, dtype) for shape, dtype in shapes],
        in_specs=specs,
        out_specs=out_specs or [VMEM] * len(shapes),
        scratch_shapes=list(scratch),
        compiler_params=pltpu.CompilerParams(vmem_limit_bytes=mib * 2**20),
        cost_estimate=pl.CostEstimate(
            flops=flops, bytes_accessed=2**20, transcendentals=0
        ),
        input_output_aliases=aliases,
        name=name,
    )(*args)


def weight_rows(where, down, out, sems, chunk, chunks):
    step = out.shape[0] // 2
    copies = []
    for core in range(2):
        at = (2 * (1 - where[X_HI]) + core) * (step * chunks) + chunk * step
        copies.append(
            pltpu.make_async_copy(
                down.at[pl.ds(pl.multiple_of(at, 16), step)],
                out.at[pl.ds(core * step, step)],
                sems.at[core],
            )
        )
        copies[-1].start()
    return copies


def pack_kernel(where, piece, near, far, cross, other, own, hidden, same, out, tokens, sems):
    x_hi = where[X_HI]
    copies = [
        pltpu.make_async_copy(own, out.at[0, 0], sems.at[0]),
        pltpu.make_async_copy(hidden, tokens.at[x_hi], sems.at[1]),
    ]
    for copy in copies:
        copy.start()
    out[0, 1] = far[...]
    out[1, 0] = near[...]
    out[1, 1] = cross[...]
    tokens[1 - x_hi] = other[...]
    for copy in copies:
        copy.wait()


def next_kernel(chunk, chunks, where, down, *refs):
    rows, sems = refs[-2:]
    for copy in weight_rows(where, down, rows, sems, chunk, chunks):
        copy.wait()


def gradient_rows(where, pieces, rows):
    for i, piece in enumerate(pieces):
        for a in range(2):
            block = where[2 * i + a]
            rows[block, :, :512] = piece[a, 0]
            rows[block, :, 512:] = piece[a, 1]


def feature_sum(chunk, chunks, where, down, got, rows, core, buf, sem, put):
    units = buf.shape[0]
    at = (2 * where[X_HI] + core) * (units * chunks) + chunk * units
    at = pl.multiple_of(at, 16)
    copy = pltpu.make_async_copy(down.at[pl.ds(at, units)], buf, sem)
    copy.start()
    copy.wait()
    inner = pl.multiple_of(core * units, 16)
    for pair in ((4, 3), (5, 2), (6, 1), (7, 0)):
        tokens = jnp.concatenate(
            [rows[lax.rem(where[ZED] + where[SIGN] * k + Z, Z)] for k in pair]
        )
        total = None
        for b, weights in enumerate((buf[...], got[pl.ds(inner, units), :])):
            part = lax.dot_general(
                weights,
                tokens[:, b * 512 : b * 512 + 512],
                (((1,), (1,)), ((), ())),
                preferred_element_type=F32,
            )
            total = part if total is None else total + part
        for i, k in enumerate(pair):
            put(k, total[:, i * 128 : i * 128 + 128])


FIRST, REST = (4, 3, 5), (2, 6, 1, 7, 0)


def rows_kernel(where, p0, p1, p2, p3, *refs):
    gradient_rows(where, (p0, p1, p2, p3), refs[-1])


def mate_kernel(chunk, chunks, where, down, got, rows, *refs):
    first, rest, buf, sem = refs[-4:]
    def put(k, value):
        if k in FIRST:
            first[FIRST.index(k)] = value
        else:
            rest[REST.index(k)] = value

    feature_sum(chunk, chunks, where, down, got, rows, 1 - where[CORE], buf, sem, put)


def own_kernel(chunk, chunks, where, down, got, rows, *refs):
    out, buf, sem = refs[-3:]

    def put(k, value):
        out[k] = value

    feature_sum(chunk, chunks, where, down, got, rows, where[CORE], buf, sem, put)


def part_of(part, size):
    return slice(part * size, part * size + size)


def send1_kernel(part, own, first, *refs):
    left, right = refs[-2:]
    half = left.shape[0]
    lower, upper = part_of(2 * part, half), part_of(2 * part + 1, half)
    left[...] = own[4, lower] + first[0, lower]
    right[...] = own[4, upper] + first[0, upper]


def send2_kernel(part, own, first, came_left, came_right, *refs):
    left, right = refs[-2:]
    half = came_left.shape[0]
    lower, upper = part_of(2 * part, half), part_of(2 * part + 1, half)
    left[:half] = own[3, lower] + first[1, lower]
    left[half:] = own[3, upper] + first[1, upper] + came_right[...]
    right[:half] = own[5, lower] + first[2, lower] + came_left[...]
    right[half:] = own[5, upper] + first[2, upper]


def send3_kernel(part, own, rest, came_left, came_right, *refs):
    left, right, near, far, base = refs[-5:]
    at = part_of(part, left.shape[0])
    left[...] = own[2, at] + rest[0, at] + came_right[...]
    right[...] = own[6, at] + rest[1, at] + came_left[...]
    near[...] = own[1, at] + rest[2, at]
    far[...] = own[7, at] + rest[3, at]
    base[...] = own[0, at] + rest[4, at]


def send4_kernel(part, near, far, came_left, came_right, *refs):
    left, right = refs[-2:]
    left[...] = near[...] + came_right[...]
    right[...] = far[...] + came_left[...]


def last_kernel(*refs):
    out = refs[-1]
    for part in range(PARTS):
        base, came_left, came_right = refs[3 * part : 3 * part + 3]
        out[part_of(part, base.shape[0])] = base[...] + came_left[...] + came_right[...]


TILES = [(0, 512), (512, 512), (1024, 512), (1536, 512), (2048, 512), (2560, 768)]


def weight_kernel(where, rows, *refs):
    hiddens, out, mark = refs[:16], refs[16], refs[17]
    g_buf, o_buf, o_sem = refs[18:]
    row = 0
    for side in range(2):
        core = where[CORE] if side == 0 else 1 - where[CORE]
        for k in (0, 1, 2, 3, -1, -2, -3, 4):
            block = lax.rem(where[ZED] + k * where[SIGN] + Z, Z)
            for x_hi in range(2):
                at = pl.multiple_of(x_hi * 64 + core * 32, 32)
                g_buf[row : row + 32] = rows[block, pl.ds(at, 32), :512]
                row += 32
    stores = []
    for i, (at, size) in enumerate(TILES):
        lines = jnp.concatenate(
            [h[:, :, at : at + size].reshape(64, size) for h in hiddens], axis=0
        )
        o_buf[at : at + size] = lax.dot_general(
            lines, g_buf[...], (((0,), (0,)), ((), ())), preferred_element_type=F32
        ).astype(BF16)
        store = pltpu.make_async_copy(
            o_buf.at[pl.ds(at, size)], out.at[pl.ds(at, size)], o_sem.at[i]
        )
        store.start()
        stores.append(store)
    mark[...] = g_buf[:16, :128]
    for store in stores:
        store.wait()


def on_device(hidden, grad_out, down_weight):
    r, c = lax.axis_index("row"), lax.axis_index("col")
    z, q = c // 4, c % 4
    x_hi, core = q // 2, q % 2
    sign = 1 - 2 * (z % 2)
    width = down_weight.shape[0]
    units = width // 4
    where = jnp.stack(
        [(r ^ m) ^ (4 * a) for m in (0, 1, 3, 2) for a in range(2)] + [q, z, core, sign, x_hi]
    ).astype(jnp.int32)

    step = units // CHUNKS
    two_sems = [pltpu.SemaphoreType.DMA((2,))]
    near = row_flip(grad_out, 4)
    cross = both_flip(grad_out, 4, 2)
    far = col_flip(grad_out, 2)
    other = col_flip(hidden, 2)
    piece = lax.dynamic_slice_in_dim(down_weight, (1 - x_hi) * 2 * units, 2 * units, 0)
    piece, mine, tokens = call(
        pack_kernel,
        "pack",
        [(piece.shape, BF16), ((2, 2, 128, 512), BF16), ((2, 32, width), BF16)],
        [SMEM, ANY] + [VMEM] * 4 + [HBM] * 2,
        (where, piece, near, far, cross, other, grad_out, hidden),
        out_specs=[ANY, VMEM, VMEM],
        scratch=two_sems,
        mib=PACK,
        aliases={1: 0},
    )
    got = [col_flip(piece, 2)]
    y1, y3 = row_flip(mine, 1), row_flip(mine, 3)
    y2 = row_flip(y1, 3)
    lefts, rights = [tokens], [tokens]
    for _ in range(3):
        left, right = z_swap(rights[-1], 0), z_swap(lefts[-1], 1)
        lefts.append(left)
        rights.append(right)
    for j in range(1, CHUNKS):
        (piece,) = call(
            functools.partial(next_kernel, j, CHUNKS),
            "next_rows",
            [((2 * step, 512), BF16)],
            [SMEM, ANY] + [VMEM] * 3,
            (where, down_weight, y1, lefts[1], rights[1]),
            scratch=two_sems,
        )
        got.append(col_flip(piece, 2))
    hiddens = lefts + rights[1:] + [z_swap(rights[-1], 0)]
    hiddens += [col_flip(h, 1) for h in hiddens]

    buffers = [pltpu.VMEM((step, 512), BF16), pltpu.SemaphoreType.DMA]
    flops = 2 * step * 1024 * 1024
    (rows,) = call(
        rows_kernel,
        "rows",
        [((8, 128, 1024), BF16)],
        [SMEM] + [VMEM] * 6,
        (where, mine, y1, y3, y2, lefts[TIED], rights[TIED]),
        flops=5 * 10**9,
    )

    def sums(j, *before):
        first, rest = call(
            functools.partial(mate_kernel, j, CHUNKS),
            "mate_sums",
            [((3, step, 128), F32), ((5, step, 128), F32)],
            [SMEM, ANY] + [VMEM] * 4,
            (where, down_weight, got[j], rows, lefts[3], rights[3]),
            scratch=buffers,
            flops=flops,
        )
        (own,) = call(
            functools.partial(own_kernel, j, CHUNKS),
            "own_sums",
            [((8, step, 128), F32)],
            [SMEM, ANY, VMEM, VMEM] + [VMEM] * len(before),
            (where, down_weight, got[j], rows, *before),
            scratch=buffers,
            flops=flops,
        )
        return own, col_flip(first, 1), col_flip(rest, 1)

    weight_grad, mark = call(
        weight_kernel,
        "weight_sum",
        [((width, 512), BF16), ((16, 128), BF16)],
        [SMEM] + [VMEM] * 17,
        (where, rows, *hiddens),
        out_specs=[ANY, VMEM],
        scratch=[
            pltpu.VMEM((1024, 512), BF16),
            pltpu.VMEM((width, 512), BF16),
            pltpu.SemaphoreType.DMA((len(TILES),)),
        ],
        mib=16,
        flops=2 * 1024 * width * 512,
    )

    def send(kernel, name, part, size, *args, kept=0):
        left, right, *others = call(
            functools.partial(kernel, part),
            name,
            [((size, 128), F32)] * (2 + kept),
            [VMEM] * len(args),
            args,
        )
        return [z_swap(left, 0), z_swap(right, 1), *others]

    def ties(stage, part):
        third = (lefts[3], rights[3]) if (stage, part) == THIRD else ()
        return third + ((hiddens[7],) if (stage, part) == FOURTH else ())

    quarters = []
    size = step // PARTS
    for j in range(CHUNKS):
        own, first, rest = sums(j, *ties(0, 0))
        parts = range(PARTS)
        got1 = [send(send1_kernel, "send1", p, size // 2, own, first, *ties(1, p)) for p in parts]
        got2 = [send(send2_kernel, "send2", p, size, own, first, *got1[p], *ties(2, p)) for p in parts]
        got3 = [send(send3_kernel, "send3", p, size, own, rest, *got2[p], *ties(3, p), kept=3) for p in parts]
        came = []
        for p in parts:
            left, right, near, far, base = got3[p]
            tie = (mark,) if p == PARTS - 1 else ()
            came += [base, *send(send4_kernel, "send4", p, size, near, far, left, right, *tie)]
        (total,) = call(
            last_kernel, "last", [((step, 128), F32)], [VMEM] * len(came), came
        )
        total = total.astype(BF16).T.reshape(2, 64, step)
        kept = lax.dynamic_index_in_dim(total, x_hi, 0, keepdims=False)
        came = col_flip(lax.dynamic_index_in_dim(total, 1 - x_hi, 0, keepdims=False), 2)
        pair = jnp.stack([jnp.where(x_hi == 0, kept, came), jnp.where(x_hi == 0, came, kept)])
        pair = pair.reshape(2, 2, 32, step)
        kept = lax.dynamic_index_in_dim(pair, core, 1, keepdims=False)
        came = col_flip(lax.dynamic_index_in_dim(pair, 1 - core, 1, keepdims=False), 1)
        one, two = jnp.where(core == 0, kept, came), jnp.where(core == 0, came, kept)
        quarters.append([one[0], two[0], one[1], two[1]])
    hidden_grad = jnp.concatenate([h[t] for t in range(4) for h in quarters], axis=1)
    return weight_grad, hidden_grad


def solution(mesh):
    in_specs = (P("col", "row"), P("row", "col"), P("row", "col"))
    out_specs = (P("row", "col"), P("col", "row"))
    return jax.shard_map(
        on_device, mesh=mesh, in_specs=in_specs, out_specs=out_specs, check_vma=False
    )
```
